512 devices in a mesh: dev: 128 (over y, z, core), band: 4 (over x).
Axes of the slice: x: 4, y: 8, z: 8, core: 2. Of those that a mesh axis runs over, the one named last changes fastest.
Arguments:
- embeddings: bfloat16 [1048576, 1024], P(('band', 'dev')), parts along dimension 0, may hold values from -6 to 6
- pair_local: int32 [512], P(('band', 'dev')), parts along dimension 0, may hold values from 0 to 1
- pair_remote: int32 [512], P(('band', 'dev')), parts along dimension 0, may hold values from 0 to 1
- pair_live: int32 [512], P(('band', 'dev')), parts along dimension 0, may hold values from 0 to 1, as said below
Outputs:
- best: float32 [1024, 1024], P(('band', 'dev')), parts along dimension 0
The draws below stay inside these ranges and needn't reach their ends.
There are 4 independent parts, one for each index of `band`. The reference program is written for one: setup_inputs(seed, part) draws one part's arguments, and reference() takes and returns one part's arrays. A program takes and returns all parts, laid end to end along the dimension named above; each array names one. Nothing has to cross between parts.
Inputs may be any that keep to these rules, and one draw needn't show every extreme that they name: pair_live is 0 wherever the partner device index i + o would reach 128 or beyond; all slots of device 0 are live.
All inputs are finite; a program needn't handle non-finite values.
Results may differ from the reference program's by a relative error of at most 0.0013.
Values may be sent and summed in bfloat16 or wider, within the bound.
A program may use at most 64 MiB of HBM per device.

```python
import jax
import jax.numpy as jnp
from jax import lax

D = 1024
BLK = 1024
BD = 2
SPAN = 2
CAP = 1
TPD = 64
ROWS = 262144
SLOTS = 128
N_DEV = 128


def draw_embeddings(key, part):
    key = jax.random.fold_in(key, 11)
    keys = jax.random.split(key, 5)
    device = jnp.arange(ROWS, dtype=jnp.int32) // (BD * BLK)
    anchor = jnp.maximum(device - jax.random.randint(keys[0], (ROWS,), 0, SPAN), 0)
    topic = anchor * TPD + jax.random.randint(keys[1], (ROWS,), 0, TPD)
    table = jax.random.normal(keys[2], (N_DEV * TPD, D), jnp.float32)
    noise = jax.random.normal(keys[3], (ROWS, D), jnp.float32)
    mixing = jax.random.uniform(keys[4], (ROWS, 1), jnp.float32, 0.1, 0.9)
    values = jnp.sqrt(mixing) * table[topic] + jnp.sqrt(1.0 - mixing) * noise
    return jnp.clip(values, -6.0, 6.0).astype(jnp.bfloat16)


def draw_pair_live(key, part):
    key = jax.random.fold_in(key, 23)
    per_device = (SPAN - 1) * CAP
    index = jnp.arange(N_DEV * per_device, dtype=jnp.int32)
    device = index // per_device
    offset = index // CAP % (SPAN - 1) + 1
    coin = jax.random.randint(key, (N_DEV * per_device,), 0, 5)
    live = (coin < 3) & (device + offset < N_DEV) | (device == 0)
    return live.astype(jnp.int32)


def plant(entries, stream_key, smallest, top_value):
    longest = entries.shape.index(max(entries.shape))
    spots = []
    for shift in (0, 1):
        where = [jax.random.randint(jax.random.fold_in(stream_key, axis), (), 0, length) for axis, length in enumerate(entries.shape)]
        where[longest] = (where[longest] + shift) % entries.shape[longest]
        spots.append(tuple(where))
    return entries.at[spots[0]].set(smallest).at[spots[1]].set(top_value)


def setup_inputs(seed: int = 0, part: int = 0) -> dict:
    key_list = jax.random.split(jax.random.key(seed), 5)
    part_keys = jax.random.split(jax.random.fold_in(key_list[4], part), 5)
    return {
        "embeddings": draw_embeddings(jax.random.fold_in(jax.random.fold_in(key_list[4], part), 71), part),
        "pair_local": plant(jax.random.randint(part_keys[1], (SLOTS,), 0, BD), jax.random.fold_in(part_keys[1], 1), 0, BD - 1).astype(jnp.int32),
        "pair_remote": plant(jax.random.randint(part_keys[2], (SLOTS,), 0, BD), jax.random.fold_in(part_keys[2], 1), 0, BD - 1).astype(jnp.int32),
        "pair_live": draw_pair_live(jax.random.fold_in(jax.random.fold_in(key_list[4], part), 71), part),
    }


def reference(embeddings, pair_local, pair_remote, pair_live):
    rows = embeddings.astype(jnp.float32)
    normed = (rows * lax.rsqrt(lax.optimization_barrier(jnp.sum(rows * rows, axis=1, keepdims=True)) + 1e-06)).astype(jnp.bfloat16)
    blocks = normed.reshape(N_DEV * BD, BLK, D)
    diagonal = jnp.eye(BLK, dtype=bool)

    def own_max(block):
        values = block.astype(jnp.float32)
        gram = jnp.dot(values, values.T, precision=lax.Precision.HIGHEST)
        return lax.optimization_barrier(jnp.max(jnp.where(diagonal, -2.0, gram), axis=1))
    best = lax.map(own_max, blocks)
    per_device = (SPAN - 1) * CAP
    index = jnp.arange(N_DEV * per_device, dtype=jnp.int32)
    device = index // per_device
    offset = index // CAP % (SPAN - 1) + 1
    first = (device * BD + pair_local).astype(jnp.int32)
    second = (jnp.minimum(device + offset, N_DEV - 1) * BD + pair_remote).astype(jnp.int32)

    def pair_max(items):
        left, right, live = items
        gram = jnp.dot(blocks[left].astype(jnp.float32), blocks[right].astype(jnp.float32).T, precision=lax.Precision.HIGHEST)
        row_best = jnp.where(live > 0, lax.optimization_barrier(jnp.max(gram, axis=1)), -2.0)
        col_best = jnp.where(live > 0, lax.optimization_barrier(jnp.max(gram, axis=0)), -2.0)
        return (row_best, col_best)
    row_best, col_best = lax.map(pair_max, (first, second, pair_live))
    best = best.at[first].max(row_best)
    best = best.at[second].max(col_best)
    return best
```

```python
import functools

import jax
import jax.numpy as jnp
from jax import lax
from jax.experimental import pallas as pl
from jax.experimental.pallas import tpu as pltpu
from jax.sharding import PartitionSpec as P

BLK = 1024
D = 1024
ROUNDS = 8
CHUNK = BLK // ROUNDS
DIRECT = 64
RELAY = 32
SPLIT_ROUNDS = 7
OWN = 256
LINE = 8
PAIR = 256
MESH = pl.DeviceIdType.MESH


def kernel(
    n_dev,
    n_band,
    local_ref,
    remote_ref,
    live_ref,
    x_hbm,
    best_ref,
    sent_ref,
    xn,
    send_buf,
    recv_buf,
    relay_buf,
    meta_out,
    meta_in,
    ret_out,
    ret_in,
    own_acc,
    pair_acc,
    load_sem,
    meta_sem,
    ret_sem,
    direct_send,
    direct_recv,
    leg1_send,
    leg1_recv,
    leg2_send,
    leg2_recv,
):
    d = lax.axis_index("dev")
    b = lax.axis_index("band")
    c = d % 2
    odd = b % 2
    step = 1 - 2 * odd
    is_s = c == 1 - odd
    is_r = c == odd
    crosses = jnp.where(c == 1, d < n_dev - 1, d > 0)
    s_cross = jnp.logical_and(is_s, crosses)
    r_cross = jnp.logical_and(is_r, crosses)
    other = d + 1 - 2 * c
    across = jnp.where(crosses, d - 1 + 2 * c, other)
    target = jnp.clip(d + step, 0, n_dev - 1)
    source = jnp.clip(d - step, 0, n_dev - 1)
    bands = (lax.rem(b + 1, n_band), lax.rem(b + n_band - 1, n_band))
    has_target = jnp.logical_or(is_r, crosses)
    has_source = jnp.logical_or(is_s, crosses)

    def load(t):
        rows = pl.ds(pl.multiple_of(t * CHUNK, CHUNK), CHUNK)
        return pltpu.make_async_copy(x_hbm.at[:, rows], xn.at[:, rows], load_sem.at[t])

    for t in range(ROUNDS):
        load(t).start()

    barrier = pltpu.get_barrier_semaphore()

    def greet(dev, band):
        pl.semaphore_signal(barrier, inc=1, device_id=(dev, band), device_id_type=MESH)

    greet(other, b)

    @pl.when(crosses)
    def _():
        greet(across, b)
        for band in bands:
            greet(d, band)

    @pl.when(r_cross)
    def _():
        for band in bands:
            greet(across, band)

    own_acc[...] = jnp.full(own_acc.shape, -2.0, jnp.float32)
    pair_acc[...] = jnp.full(pair_acc.shape, -2.0, jnp.float32)

    def normalize(t, carry):
        rows = pl.ds(pl.multiple_of(t * CHUNK, CHUNK), CHUNK)
        load(t).wait()
        for k in range(2):
            values = xn[k, rows].astype(jnp.float32)
            scale = lax.rsqrt(jnp.sum(values * values, axis=1, keepdims=True) + 1e-06)
            xn[k, rows] = (values * scale).astype(jnp.bfloat16)
        return carry

    early = jnp.where(d // 2 % LINE == LINE - 1, 0, ROUNDS)
    lax.fori_loop(0, early, normalize, 0)

    row = lax.broadcasted_iota(jnp.int32, (8, 128), 0)
    meta_out[...] = jnp.where(row == 0, remote_ref[0], live_ref[0])

    def own(t, carry):
        k = t % 2
        first = pl.multiple_of(t // 2 * OWN, OWN)
        gram = lax.dot_general(
            xn[k, pl.ds(first, OWN)],
            xn[k],
            (((1,), (1,)), ((), ())),
            preferred_element_type=jnp.float32,
        )
        rows = lax.broadcasted_iota(jnp.int32, gram.shape, 0) + first
        columns = lax.broadcasted_iota(jnp.int32, gram.shape, 1)
        gram = jnp.where(rows == columns, -2.0, gram)
        own_acc[k] = jnp.maximum(own_acc[k], jnp.max(gram.reshape(OWN // 8, 8, BLK), axis=0))
        return carry

    lax.fori_loop(0, early, own, 0)

    waits = 1 + jnp.where(crosses, 3, 0) + jnp.where(r_cross, 2, 0)
    pl.semaphore_wait(barrier, waits)

    meta_copy = pltpu.make_async_remote_copy(
        src_ref=meta_out,
        dst_ref=meta_in,
        send_sem=meta_sem.at[0],
        recv_sem=meta_sem.at[1],
        device_id=(jnp.minimum(d + 1, n_dev - 1), b),
        device_id_type=MESH,
    )

    @pl.when(d < n_dev - 1)
    def _():
        meta_copy.start()

    def piece(t, start, size):
        return pl.ds(pl.multiple_of(t * CHUNK + start, 16), size)

    def direct(t, size):
        rows = piece(t, 0, size)
        return pltpu.make_async_remote_copy(
            src_ref=send_buf.at[rows],
            dst_ref=recv_buf.at[rows],
            send_sem=direct_send.at[t],
            recv_sem=direct_recv.at[t],
            device_id=(target, b),
            device_id_type=MESH,
        )

    def relay_rows(t, side):
        return piece(t, DIRECT + side * RELAY, RELAY)

    def leg1(t, side):
        return pltpu.make_async_remote_copy(
            src_ref=send_buf.at[relay_rows(t, side)],
            dst_ref=relay_buf.at[side, pl.ds(pl.multiple_of(t * RELAY, RELAY), RELAY)],
            send_sem=leg1_send.at[side, t],
            recv_sem=leg1_recv.at[side, t],
            device_id=(d, bands[side]),
            device_id_type=MESH,
        )

    def leg2(t, side):
        return pltpu.make_async_remote_copy(
            src_ref=relay_buf.at[side, pl.ds(pl.multiple_of(t * RELAY, RELAY), RELAY)],
            dst_ref=recv_buf.at[relay_rows(t, side)],
            send_sem=leg2_send.at[side, t],
            recv_sem=leg2_recv.at[side, t],
            device_id=(across, bands[1 - side]),
            device_id_type=MESH,
        )

    def forward(t):
        for side in range(2):
            leg1(t, side).wait_recv()
            leg2(t, side).start()

    def send(t, index):
        rows = piece(t, 0, CHUNK)
        send_buf[rows] = jnp.where(index == 0, xn[0, rows], xn[1, rows])

        @pl.when(is_r)
        def _():
            direct(t, CHUNK).start()

        @pl.when(s_cross)
        def _():
            @pl.when(t < SPLIT_ROUNDS)
            def _():
                for side in range(2):
                    leg1(t, side).start()
                direct(t, DIRECT).start()

            @pl.when(t >= SPLIT_ROUNDS)
            def _():
                direct(t, CHUNK).start()

    def send_all(index):
        def body(t, carry):
            @pl.when(t >= early)
            def _():
                normalize(t, 0)

            send(t, index)
            return carry

        lax.fori_loop(0, ROUNDS, body, 0)

    def learn():
        @pl.when(d > 0)
        def _():
            meta_copy.wait_recv()

        @pl.when(d == 0)
        def _():
            meta_in[...] = jnp.zeros_like(meta_in)

    @pl.when(odd == 0)
    def _():
        send_all(local_ref[0])
        learn()

    @pl.when(odd == 1)
    def _():
        learn()
        send_all(meta_in[0, 0])

    before_remote = meta_in[0, 0]
    before_live = meta_in[1, 0]
    forwards = odd == 0
    send_index = jnp.where(forwards, local_ref[0], before_remote)
    send_live = jnp.where(forwards, live_ref[0], before_live)
    keep_index = jnp.where(forwards, before_remote, local_ref[0])
    keep_live = jnp.where(forwards, before_live, live_ref[0])

    def relay(t, carry):
        @pl.when(t >= early)
        def _():
            own(t, 0)

        @pl.when(jnp.logical_and(r_cross, t < SPLIT_ROUNDS))
        def _():
            forward(t)

        return carry

    lax.fori_loop(0, ROUNDS, relay, 0)

    def arrive(t):
        @pl.when(jnp.logical_or(is_s, t >= SPLIT_ROUNDS))
        def _():
            direct(t, CHUNK).wait_recv()

        @pl.when(jnp.logical_and(is_r, t < SPLIT_ROUNDS))
        def _():
            direct(t, DIRECT).wait_recv()
            for side in range(2):
                leg2(t, side).wait_recv()

    def pair(t):
        rows = pl.ds(pl.multiple_of(t * PAIR, PAIR), PAIR)
        gram = lax.dot_general(
            recv_buf[rows],
            xn[keep_index],
            (((1,), (1,)), ((), ())),
            preferred_element_type=jnp.float32,
        )
        pair_acc[...] = jnp.maximum(
            pair_acc[...], jnp.max(gram.reshape(PAIR // 8, 8, BLK), axis=0)
        )
        narrow = gram[:, :128]
        for j in range(1, BLK // 128):
            narrow = jnp.maximum(narrow, gram[:, j * 128 : (j + 1) * 128])
        for j in range(PAIR // 128):
            part = jnp.max(narrow[j * 128 : (j + 1) * 128].T, axis=0, keepdims=True)
            ret_out[pl.ds(t * (PAIR // 128) + j, 1)] = part

    def compare(t, carry):
        for j in range(PAIR // CHUNK):
            arrive(t * (PAIR // CHUNK) + j)
        pair(t)
        return carry

    @pl.when(has_source)
    def _():
        lax.fori_loop(0, BLK // PAIR, compare, 0)

    ret_copy = pltpu.make_async_remote_copy(
        src_ref=ret_out,
        dst_ref=ret_in,
        send_sem=ret_sem.at[0],
        recv_sem=ret_sem.at[1],
        device_id=(source, b),
        device_id_type=MESH,
    )

    @pl.when(has_source)
    def _():
        ret_copy.start()

    @pl.when(has_target)
    def _():
        ret_copy.wait_recv()

    @pl.when(jnp.logical_not(has_target))
    def _():
        ret_in[...] = jnp.full(ret_in.shape, -2.0, jnp.float32)

    kept = jnp.max(pair_acc[...], axis=0, keepdims=True)
    kept = jnp.where(keep_live > 0, kept, -2.0)
    sent = jnp.concatenate([ret_in[t : t + 1] for t in range(ROUNDS)], axis=1)
    sent = jnp.where(send_live > 0, sent, -2.0)
    for k in range(2):
        best = jnp.max(own_acc[k], axis=0, keepdims=True)
        best_ref[k : k + 1] = jnp.maximum(best, jnp.where(keep_index == k, kept, -2.0))
        sent_ref[k : k + 1] = jnp.where(send_index == k, sent, -2.0)

    @pl.when(d < n_dev - 1)
    def _():
        meta_copy.wait_send()

    @pl.when(has_source)
    def _():
        ret_copy.wait_send()

    def drain(t, carry):
        @pl.when(jnp.logical_or(is_r, jnp.logical_and(crosses, t >= SPLIT_ROUNDS)))
        def _():
            direct(t, CHUNK).wait_send()

        @pl.when(jnp.logical_and(s_cross, t < SPLIT_ROUNDS))
        def _():
            direct(t, DIRECT).wait_send()
            for side in range(2):
                leg1(t, side).wait_send()

        @pl.when(jnp.logical_and(r_cross, t < SPLIT_ROUNDS))
        def _():
            for side in range(2):
                leg2(t, side).wait_send()

        return carry

    lax.fori_loop(0, ROUNDS, drain, 0)


def solution(mesh):
    n_dev, n_band = mesh.shape["dev"], mesh.shape["band"]
    dma = pltpu.SemaphoreType.DMA

    def local(embeddings, pair_local, pair_remote, pair_live):
        blocks = embeddings.reshape(2, BLK, D)
        best, sent = pl.pallas_call(
            functools.partial(kernel, n_dev, n_band),
            out_shape=[jax.ShapeDtypeStruct((2, BLK), jnp.float32)] * 2,
            in_specs=[pl.BlockSpec(memory_space=pltpu.SMEM)] * 3
            + [pl.BlockSpec(memory_space=pl.ANY)],
            out_specs=[pl.BlockSpec(memory_space=pltpu.VMEM)] * 2,
            scratch_shapes=[
                pltpu.VMEM((2, BLK, D), jnp.bfloat16),
                pltpu.VMEM((BLK, D), jnp.bfloat16),
                pltpu.VMEM((BLK, D), jnp.bfloat16),
                pltpu.VMEM((2, ROUNDS * RELAY, D), jnp.bfloat16),
                pltpu.VMEM((8, 128), jnp.int32),
                pltpu.VMEM((8, 128), jnp.int32),
                pltpu.VMEM((ROUNDS, CHUNK), jnp.float32),
                pltpu.VMEM((ROUNDS, CHUNK), jnp.float32),
                pltpu.VMEM((2, 8, BLK), jnp.float32),
                pltpu.VMEM((8, BLK), jnp.float32),
                dma((ROUNDS,)),
                dma((2,)),
                dma((2,)),
                dma((ROUNDS,)),
                dma((ROUNDS,)),
                dma((2, ROUNDS)),
                dma((2, ROUNDS)),
                dma((2, ROUNDS)),
                dma((2, ROUNDS)),
            ],
            compiler_params=pltpu.CompilerParams(
                collective_id=1, has_side_effects=True, vmem_limit_bytes=52 << 20
            ),
            cost_estimate=pl.CostEstimate(
                flops=6 * BLK * BLK * D, bytes_accessed=4 * BLK * D, transcendentals=0
            ),
        )(pair_local, pair_remote, pair_live, blocks)
        return jnp.maximum(best, sent)

    placed = (P(("band", "dev"), None), P(("band", "dev")), P(("band", "dev")), P(("band", "dev")))
    return jax.shard_map(
        local, mesh=mesh, in_specs=placed, out_specs=P(("band", "dev"), None), check_vma=False
    )
```

```python
import functools

import jax
import jax.numpy as jnp
from jax import lax
from jax.experimental import pallas as pl
from jax.experimental.pallas import tpu as pltpu
from jax.sharding import PartitionSpec as P

BLK = 1024
D = 1024
ROUNDS = 8
CHUNK = BLK // ROUNDS
DIRECT = 64
RELAY = 32
SPLIT_ROUNDS = 6
OWN = 256
LINE = 8
AHEAD = 6
BEFORE = 4
PAIR = 256
MESH = pl.DeviceIdType.MESH


def kernel(
    n_dev,
    n_band,
    local_ref,
    remote_ref,
    live_ref,
    x_hbm,
    best_ref,
    sent_ref,
    xn,
    send_buf,
    recv_buf,
    relay_buf,
    meta_out,
    meta_in,
    ret_out,
    ret_in,
    own_acc,
    pair_acc,
    load_sem,
    meta_sem,
    ret_sem,
    direct_send,
    direct_recv,
    leg1_send,
    leg1_recv,
    leg2_send,
    leg2_recv,
):
    d = lax.axis_index("dev")
    b = lax.axis_index("band")
    c = d % 2
    odd = b % 2
    step = 1 - 2 * odd
    is_s = c == 1 - odd
    is_r = c == odd
    crosses = jnp.where(c == 1, d < n_dev - 1, d > 0)
    s_cross = jnp.logical_and(is_s, crosses)
    r_cross = jnp.logical_and(is_r, crosses)
    other = d + 1 - 2 * c
    across = jnp.where(crosses, d - 1 + 2 * c, other)
    target = jnp.clip(d + step, 0, n_dev - 1)
    source = jnp.clip(d - step, 0, n_dev - 1)
    bands = (lax.rem(b + 1, n_band), lax.rem(b + n_band - 1, n_band))
    has_target = jnp.logical_or(is_r, crosses)
    has_source = jnp.logical_or(is_s, crosses)

    def load(t):
        rows = pl.ds(pl.multiple_of(t * CHUNK, CHUNK), CHUNK)
        return pltpu.make_async_copy(x_hbm.at[:, rows], xn.at[:, rows], load_sem.at[t])

    for t in range(ROUNDS):
        load(t).start()

    barrier = pltpu.get_barrier_semaphore()

    def greet(dev, band):
        pl.semaphore_signal(barrier, inc=1, device_id=(dev, band), device_id_type=MESH)

    greet(other, b)

    @pl.when(crosses)
    def _():
        greet(across, b)

    @pl.when(r_cross)
    def _():
        for band in bands:
            greet(d, band)
            greet(across, band)

    own_acc[...] = jnp.full(own_acc.shape, -2.0, jnp.float32)
    pair_acc[...] = jnp.full(pair_acc.shape, -2.0, jnp.float32)

    def normalize(t, carry):
        rows = pl.ds(pl.multiple_of(t * CHUNK, CHUNK), CHUNK)
        load(t).wait()
        for k in range(2):
            values = xn[k, rows].astype(jnp.float32)
            scale = lax.rsqrt(jnp.sum(values * values, axis=1, keepdims=True) + 1e-06)
            xn[k, rows] = (values * scale).astype(jnp.bfloat16)
        return carry

    first = d // 2 % LINE == 0
    early = jnp.where(first, ROUNDS, 0)
    before = jnp.where(first, BEFORE, 0)
    lax.fori_loop(0, early, normalize, 0)

    row = lax.broadcasted_iota(jnp.int32, (8, 128), 0)
    meta_out[...] = jnp.where(row == 0, remote_ref[0], live_ref[0])

    def own(t, carry):
        k = t % 2
        start = pl.multiple_of(t // 2 * OWN, OWN)
        gram = lax.dot_general(
            xn[k, pl.ds(start, OWN)],
            xn[k],
            (((1,), (1,)), ((), ())),
            preferred_element_type=jnp.float32,
        )
        rows = lax.broadcasted_iota(jnp.int32, gram.shape, 0) + start
        columns = lax.broadcasted_iota(jnp.int32, gram.shape, 1)
        gram = jnp.where(rows == columns, -2.0, gram)
        own_acc[k] = jnp.maximum(own_acc[k], jnp.max(gram.reshape(OWN // 8, 8, BLK), axis=0))
        return carry

    lax.fori_loop(0, before, own, 0)

    waits = 1 + jnp.where(crosses, 3, 0)
    pl.semaphore_wait(barrier, waits)

    meta_copy = pltpu.make_async_remote_copy(
        src_ref=meta_out,
        dst_ref=meta_in,
        send_sem=meta_sem.at[0],
        recv_sem=meta_sem.at[1],
        device_id=(jnp.minimum(d + 1, n_dev - 1), b),
        device_id_type=MESH,
    )

    @pl.when(d < n_dev - 1)
    def _():
        meta_copy.start()

    def piece(t, start, size):
        return pl.ds(pl.multiple_of(t * CHUNK + start, 16), size)

    def direct(t, size):
        rows = piece(t, 0, size)
        return pltpu.make_async_remote_copy(
            src_ref=send_buf.at[rows],
            dst_ref=recv_buf.at[rows],
            send_sem=direct_send.at[t],
            recv_sem=direct_recv.at[t],
            device_id=(target, b),
            device_id_type=MESH,
        )

    def relay_rows(t, side):
        return piece(t, DIRECT + side * RELAY, RELAY)

    def leg1(t, side):
        return pltpu.make_async_remote_copy(
            src_ref=send_buf.at[relay_rows(t, side)],
            dst_ref=relay_buf.at[side, pl.ds(pl.multiple_of(t * RELAY, RELAY), RELAY)],
            send_sem=leg1_send.at[side, t],
            recv_sem=leg1_recv.at[side, t],
            device_id=(d, bands[side]),
            device_id_type=MESH,
        )

    def leg2(t, side):
        return pltpu.make_async_remote_copy(
            src_ref=relay_buf.at[side, pl.ds(pl.multiple_of(t * RELAY, RELAY), RELAY)],
            dst_ref=recv_buf.at[relay_rows(t, side)],
            send_sem=leg2_send.at[side, t],
            recv_sem=leg2_recv.at[side, t],
            device_id=(across, bands[1 - side]),
            device_id_type=MESH,
        )

    def forward(t):
        for side in range(2):
            leg1(t, side).wait_recv()
            leg2(t, side).start()

    def send(t, index):
        rows = piece(t, 0, CHUNK)
        send_buf[rows] = jnp.where(index == 0, xn[0, rows], xn[1, rows])

        @pl.when(is_r)
        def _():
            direct(t, CHUNK).start()

        @pl.when(s_cross)
        def _():
            @pl.when(t < SPLIT_ROUNDS)
            def _():
                for side in range(2):
                    leg1(t, side).start()
                direct(t, DIRECT).start()

            @pl.when(t >= SPLIT_ROUNDS)
            def _():
                direct(t, CHUNK).start()

    def send_all(index):
        def body(t, carry):
            @pl.when(t >= early)
            def _():
                normalize(t, 0)

            send(t, index)
            return carry

        lax.fori_loop(0, ROUNDS, body, 0)

    def learn():
        @pl.when(d > 0)
        def _():
            meta_copy.wait_recv()

        @pl.when(d == 0)
        def _():
            meta_in[...] = jnp.zeros_like(meta_in)

    def relay(t, carry):
        @pl.when(t >= before)
        def _():
            own(t, 0)

        @pl.when(jnp.logical_and(r_cross, t < SPLIT_ROUNDS))
        def _():
            forward(t)

        return carry

    ahead = jnp.where(jnp.logical_and(is_r, jnp.logical_and(odd == 1, first)), AHEAD, 0)
    lax.fori_loop(0, ahead, relay, 0)

    @pl.when(odd == 0)
    def _():
        send_all(local_ref[0])

    @pl.when(odd == 1)
    def _():
        learn()
        send_all(meta_in[0, 0])

    lax.fori_loop(ahead, ROUNDS, relay, 0)

    @pl.when(odd == 0)
    def _():
        learn()

    before_remote = meta_in[0, 0]
    before_live = meta_in[1, 0]
    forwards = odd == 0
    send_index = jnp.where(forwards, local_ref[0], before_remote)
    send_live = jnp.where(forwards, live_ref[0], before_live)
    keep_index = jnp.where(forwards, before_remote, local_ref[0])
    keep_live = jnp.where(forwards, before_live, live_ref[0])

    def arrive(t):
        @pl.when(jnp.logical_or(is_s, t >= SPLIT_ROUNDS))
        def _():
            direct(t, CHUNK).wait_recv()

        @pl.when(jnp.logical_and(is_r, t < SPLIT_ROUNDS))
        def _():
            direct(t, DIRECT).wait_recv()
            for side in range(2):
                leg2(t, side).wait_recv()

    def pair(t):
        rows = pl.ds(pl.multiple_of(t * PAIR, PAIR), PAIR)
        gram = lax.dot_general(
            recv_buf[rows],
            xn[keep_index],
            (((1,), (1,)), ((), ())),
            preferred_element_type=jnp.float32,
        )
        pair_acc[...] = jnp.maximum(
            pair_acc[...], jnp.max(gram.reshape(PAIR // 8, 8, BLK), axis=0)
        )
        narrow = gram[:, :128]
        for j in range(1, BLK // 128):
            narrow = jnp.maximum(narrow, gram[:, j * 128 : (j + 1) * 128])
        for j in range(PAIR // 128):
            part = jnp.max(narrow[j * 128 : (j + 1) * 128].T, axis=0, keepdims=True)
            ret_out[pl.ds(t * (PAIR // 128) + j, 1)] = part

    def compare(t, carry):
        for j in range(PAIR // CHUNK):
            arrive(t * (PAIR // CHUNK) + j)
        pair(t)
        return carry

    @pl.when(has_source)
    def _():
        lax.fori_loop(0, BLK // PAIR, compare, 0)

    ret_copy = pltpu.make_async_remote_copy(
        src_ref=ret_out,
        dst_ref=ret_in,
        send_sem=ret_sem.at[0],
        recv_sem=ret_sem.at[1],
        device_id=(source, b),
        device_id_type=MESH,
    )

    @pl.when(has_source)
    def _():
        ret_copy.start()

    @pl.when(has_target)
    def _():
        ret_copy.wait_recv()

    @pl.when(jnp.logical_not(has_target))
    def _():
        ret_in[...] = jnp.full(ret_in.shape, -2.0, jnp.float32)

    kept = jnp.max(pair_acc[...], axis=0, keepdims=True)
    kept = jnp.where(keep_live > 0, kept, -2.0)
    sent = jnp.concatenate([ret_in[t : t + 1] for t in range(ROUNDS)], axis=1)
    sent = jnp.where(send_live > 0, sent, -2.0)
    for k in range(2):
        best = jnp.max(own_acc[k], axis=0, keepdims=True)
        best_ref[k : k + 1] = jnp.maximum(best, jnp.where(keep_index == k, kept, -2.0))
        sent_ref[k : k + 1] = jnp.where(send_index == k, sent, -2.0)

    @pl.when(d < n_dev - 1)
    def _():
        meta_copy.wait_send()

    @pl.when(has_source)
    def _():
        ret_copy.wait_send()

    def drain(t, carry):
        @pl.when(jnp.logical_or(is_r, jnp.logical_and(crosses, t >= SPLIT_ROUNDS)))
        def _():
            direct(t, CHUNK).wait_send()

        @pl.when(jnp.logical_and(s_cross, t < SPLIT_ROUNDS))
        def _():
            direct(t, DIRECT).wait_send()
            for side in range(2):
                leg1(t, side).wait_send()

        @pl.when(jnp.logical_and(r_cross, t < SPLIT_ROUNDS))
        def _():
            for side in range(2):
                leg2(t, side).wait_send()

        return carry

    lax.fori_loop(0, ROUNDS, drain, 0)


def solution(mesh):
    n_dev, n_band = mesh.shape["dev"], mesh.shape["band"]
    dma = pltpu.SemaphoreType.DMA

    def local(embeddings, pair_local, pair_remote, pair_live):
        blocks = embeddings.reshape(2, BLK, D)
        best, sent = pl.pallas_call(
            functools.partial(kernel, n_dev, n_band),
            out_shape=[jax.ShapeDtypeStruct((2, BLK), jnp.float32)] * 2,
            in_specs=[pl.BlockSpec(memory_space=pltpu.SMEM)] * 3
            + [pl.BlockSpec(memory_space=pl.ANY)],
            out_specs=[pl.BlockSpec(memory_space=pltpu.VMEM)] * 2,
            scratch_shapes=[
                pltpu.VMEM((2, BLK, D), jnp.bfloat16),
                pltpu.VMEM((BLK, D), jnp.bfloat16),
                pltpu.VMEM((BLK, D), jnp.bfloat16),
                pltpu.VMEM((2, ROUNDS * RELAY, D), jnp.bfloat16),
                pltpu.VMEM((8, 128), jnp.int32),
                pltpu.VMEM((8, 128), jnp.int32),
                pltpu.VMEM((ROUNDS, CHUNK), jnp.float32),
                pltpu.VMEM((ROUNDS, CHUNK), jnp.float32),
                pltpu.VMEM((2, 8, BLK), jnp.float32),
                pltpu.VMEM((8, BLK), jnp.float32),
                dma((ROUNDS,)),
                dma((2,)),
                dma((2,)),
                dma((ROUNDS,)),
                dma((ROUNDS,)),
                dma((2, ROUNDS)),
                dma((2, ROUNDS)),
                dma((2, ROUNDS)),
                dma((2, ROUNDS)),
            ],
            compiler_params=pltpu.CompilerParams(
                collective_id=1, has_side_effects=True, vmem_limit_bytes=52 << 20
            ),
            cost_estimate=pl.CostEstimate(
                flops=6 * BLK * BLK * D, bytes_accessed=4 * BLK * D, transcendentals=0
            ),
        )(pair_local, pair_remote, pair_live, blocks)
        return jnp.maximum(best, sent)

    placed = (P(("band", "dev"), None), P(("band", "dev")), P(("band", "dev")), P(("band", "dev")))
    return jax.shard_map(
        local, mesh=mesh, in_specs=placed, out_specs=P(("band", "dev"), None), check_vma=False
    )
```

```python
import functools

import jax
import jax.numpy as jnp
from jax import lax
from jax.experimental import pallas as pl
from jax.experimental.pallas import tpu as pltpu
from jax.sharding import PartitionSpec as P

BLK = 1024
D = 1024
ROUNDS = 8
CHUNK = BLK // ROUNDS
DIRECT = 64
RELAY = 32
SPLIT_EVEN = 6
SPLIT_ODD = 6
SPEC = 48
PRE = 1
OWN = 256
LINE = 8
AHEAD = 6
BEFORE = 4
PAIR = 256
MESH = pl.DeviceIdType.MESH


def kernel(
    n_dev,
    n_band,
    local_ref,
    remote_ref,
    live_ref,
    x_hbm,
    best_ref,
    sent_ref,
    xn,
    send_buf,
    recv_buf,
    relay_buf,
    pre_buf,
    spec_buf,
    client_in,
    meta_out,
    meta_in,
    ret_out,
    ret_in,
    own_acc,
    pair_acc,
    load_sem,
    meta_sem,
    ret_sem,
    direct_send,
    direct_recv,
    leg1_send,
    leg1_recv,
    leg2_send,
    leg2_recv,
    pre_send,
    pre_recv,
    spec_send,
    spec_recv,
    client_send,
    client_recv,
):
    d = lax.axis_index("dev")
    b = lax.axis_index("band")
    c = d % 2
    odd = b % 2
    step = 1 - 2 * odd
    is_s = c == 1 - odd
    is_r = c == odd
    crosses = jnp.where(c == 1, d < n_dev - 1, d > 0)
    s_cross = jnp.logical_and(is_s, crosses)
    r_cross = jnp.logical_and(is_r, crosses)
    s_odd = jnp.logical_and(s_cross, odd == 1)
    r_odd = jnp.logical_and(r_cross, odd == 1)
    r_even = jnp.logical_and(r_cross, odd == 0)
    split = jnp.where(odd == 1, SPLIT_ODD, SPLIT_EVEN)
    skip = jnp.where(odd == 1, PRE, 0)
    relayed = jnp.where(odd == 1, SPLIT_EVEN, SPLIT_ODD)
    other = d + 1 - 2 * c
    across = jnp.where(crosses, d - 1 + 2 * c, other)
    target = jnp.clip(d + step, 0, n_dev - 1)
    source = jnp.clip(d - step, 0, n_dev - 1)
    bands = (lax.rem(b + 1, n_band), lax.rem(b + n_band - 1, n_band))
    has_target = jnp.logical_or(is_r, crosses)
    has_source = jnp.logical_or(is_s, crosses)

    def load(t):
        rows = pl.ds(pl.multiple_of(t * CHUNK, CHUNK), CHUNK)
        return pltpu.make_async_copy(x_hbm.at[:, rows], xn.at[:, rows], load_sem.at[t])

    for t in range(ROUNDS):
        load(t).start()

    barrier = pltpu.get_barrier_semaphore()

    def greet(dev, band):
        pl.semaphore_signal(barrier, inc=1, device_id=(dev, band), device_id_type=MESH)

    greet(other, b)

    @pl.when(crosses)
    def _():
        greet(across, b)

    @pl.when(r_cross)
    def _():
        for band in bands:
            greet(d, band)
            greet(across, band)

    own_acc[...] = jnp.full(own_acc.shape, -2.0, jnp.float32)
    pair_acc[...] = jnp.full(pair_acc.shape, -2.0, jnp.float32)

    def normalize(t, carry):
        rows = pl.ds(pl.multiple_of(t * CHUNK, CHUNK), CHUNK)
        load(t).wait()
        for k in range(2):
            values = xn[k, rows].astype(jnp.float32)
            scale = lax.rsqrt(jnp.sum(values * values, axis=1, keepdims=True) + 1e-06)
            xn[k, rows] = (values * scale).astype(jnp.bfloat16)
        return carry

    first = d // 2 % LINE == 0
    early = jnp.where(first, ROUNDS, 0)
    before = jnp.where(first, BEFORE, 0)
    lax.fori_loop(0, early, normalize, 0)

    row = lax.broadcasted_iota(jnp.int32, (8, 128), 0)
    meta_out[...] = jnp.where(row == 0, remote_ref[0], live_ref[0])

    def own(t, carry):
        k = t % 2
        start = pl.multiple_of(t // 2 * OWN, OWN)
        gram = lax.dot_general(
            xn[k, pl.ds(start, OWN)],
            xn[k],
            (((1,), (1,)), ((), ())),
            preferred_element_type=jnp.float32,
        )
        rows = lax.broadcasted_iota(jnp.int32, gram.shape, 0) + start
        columns = lax.broadcasted_iota(jnp.int32, gram.shape, 1)
        gram = jnp.where(rows == columns, -2.0, gram)
        own_acc[k] = jnp.maximum(own_acc[k], jnp.max(gram.reshape(OWN // 8, 8, BLK), axis=0))
        return carry

    lax.fori_loop(0, before, own, 0)

    waits = 1 + jnp.where(crosses, 3, 0)
    pl.semaphore_wait(barrier, waits)

    meta_copy = pltpu.make_async_remote_copy(
        src_ref=meta_out,
        dst_ref=meta_in,
        send_sem=meta_sem.at[0],
        recv_sem=meta_sem.at[1],
        device_id=(jnp.minimum(d + 1, n_dev - 1), b),
        device_id_type=MESH,
    )

    @pl.when(d < n_dev - 1)
    def _():
        meta_copy.start()

    def client(side):
        return pltpu.make_async_remote_copy(
            src_ref=meta_out,
            dst_ref=client_in.at[side],
            send_sem=client_send.at[side],
            recv_sem=client_recv.at[side],
            device_id=(across, bands[side]),
            device_id_type=MESH,
        )

    @pl.when(r_odd)
    def _():
        for side in range(2):
            client(side).start()

    def piece(t, start, size):
        return pl.ds(pl.multiple_of(t * CHUNK + start, 16), size)

    def direct(t, size):
        rows = piece(t, 0, size)
        return pltpu.make_async_remote_copy(
            src_ref=send_buf.at[rows],
            dst_ref=recv_buf.at[rows],
            send_sem=direct_send.at[t],
            recv_sem=direct_recv.at[t],
            device_id=(target, b),
            device_id_type=MESH,
        )

    def relay_rows(t, side):
        return piece(t, DIRECT + side * RELAY, RELAY)

    def leg1(t, side):
        return pltpu.make_async_remote_copy(
            src_ref=send_buf.at[relay_rows(t, side)],
            dst_ref=relay_buf.at[side, pl.ds(pl.multiple_of(t * RELAY, RELAY), RELAY)],
            send_sem=leg1_send.at[side, t],
            recv_sem=leg1_recv.at[side, t],
            device_id=(d, bands[side]),
            device_id_type=MESH,
        )

    def leg2(t, side):
        return pltpu.make_async_remote_copy(
            src_ref=relay_buf.at[side, pl.ds(pl.multiple_of(t * RELAY, RELAY), RELAY)],
            dst_ref=recv_buf.at[relay_rows(t, side)],
            send_sem=leg2_send.at[side, t],
            recv_sem=leg2_recv.at[side, t],
            device_id=(across, bands[1 - side]),
            device_id_type=MESH,
        )

    def held(t):
        return pl.ds(pl.multiple_of(t * RELAY, RELAY), RELAY)

    def pre(t, side, k):
        return pltpu.make_async_remote_copy(
            src_ref=xn.at[k, relay_rows(t, side)],
            dst_ref=pre_buf.at[side, k, held(t)],
            send_sem=pre_send.at[side, k, t],
            recv_sem=pre_recv.at[side, k, t],
            device_id=(d, bands[side]),
            device_id_type=MESH,
        )

    def spec(k):
        return pltpu.make_async_remote_copy(
            src_ref=xn.at[k, pl.ds(0, SPEC)],
            dst_ref=spec_buf.at[k],
            send_sem=spec_send.at[k],
            recv_sem=spec_recv.at[k],
            device_id=(target, b),
            device_id_type=MESH,
        )

    def direct_rest():
        rows = pl.ds(SPEC, DIRECT - SPEC)
        return pltpu.make_async_remote_copy(
            src_ref=send_buf.at[rows],
            dst_ref=recv_buf.at[rows],
            send_sem=direct_send.at[0],
            recv_sem=direct_recv.at[0],
            device_id=(target, b),
            device_id_type=MESH,
        )

    def forward(t):
        @pl.when(jnp.logical_or(odd == 1, t >= PRE))
        def _():
            for side in range(2):
                leg1(t, side).wait_recv()
                leg2(t, side).start()

        @pl.when(jnp.logical_and(odd == 0, t < PRE))
        def _():
            for side in range(2):
                for k in range(2):
                    pre(t, side, k).wait_recv()
                relay_buf[side, held(t)] = jnp.where(
                    client_in[side, 0, 0] == 0,
                    pre_buf[side, 0, held(t)],
                    pre_buf[side, 1, held(t)],
                )
                leg2(t, side).start()

    def send(t, index):
        rows = piece(t, 0, CHUNK)
        send_buf[rows] = jnp.where(index == 0, xn[0, rows], xn[1, rows])

        @pl.when(is_r)
        def _():
            direct(t, CHUNK).start()

        @pl.when(jnp.logical_and(s_cross, t >= split))
        def _():
            direct(t, CHUNK).start()

        @pl.when(jnp.logical_and(s_cross, jnp.logical_and(t >= skip, t < split)))
        def _():
            for side in range(2):
                leg1(t, side).start()

        @pl.when(jnp.logical_and(jnp.logical_and(s_cross, odd == 0), t < split))
        def _():
            direct(t, DIRECT).start()

        @pl.when(jnp.logical_and(s_odd, t == 0))
        def _():
            direct_rest().start()

        @pl.when(jnp.logical_and(s_odd, jnp.logical_and(t > 0, t < split)))
        def _():
            direct(t, DIRECT).start()

    def send_all(index):
        def body(t, carry):
            @pl.when(jnp.logical_and(jnp.logical_not(s_odd), t >= early))
            def _():
                normalize(t, 0)

            send(t, index)
            return carry

        lax.fori_loop(0, ROUNDS, body, 0)

    def learn():
        @pl.when(d > 0)
        def _():
            meta_copy.wait_recv()

        @pl.when(d == 0)
        def _():
            meta_in[...] = jnp.zeros_like(meta_in)

    def relay(t, carry):
        @pl.when(t >= before)
        def _():
            own(t, 0)

        @pl.when(jnp.logical_and(r_cross, t < relayed))
        def _():
            forward(t)

        return carry

    ahead = jnp.where(jnp.logical_and(is_r, jnp.logical_and(odd == 1, first)), AHEAD, 0)
    lax.fori_loop(0, ahead, relay, 0)

    @pl.when(odd == 0)
    def _():
        send_all(local_ref[0])

    def send_both(t, carry):
        @pl.when(t >= early)
        def _():
            normalize(t, 0)

        @pl.when(t == 0)
        def _():
            for k in range(2):
                spec(k).start()

        @pl.when(t < PRE)
        def _():
            for side in range(2):
                for k in range(2):
                    pre(t, side, k).start()

        return carry

    @pl.when(s_odd)
    def _():
        lax.fori_loop(0, ROUNDS, send_both, 0)

    @pl.when(odd == 1)
    def _():
        learn()
        send_all(meta_in[0, 0])

    @pl.when(r_even)
    def _():
        for side in range(2):
            client(side).wait_recv()

    lax.fori_loop(ahead, ROUNDS, relay, 0)

    @pl.when(odd == 0)
    def _():
        learn()

    before_remote = meta_in[0, 0]
    before_live = meta_in[1, 0]
    forwards = odd == 0
    send_index = jnp.where(forwards, local_ref[0], before_remote)
    send_live = jnp.where(forwards, live_ref[0], before_live)
    keep_index = jnp.where(forwards, before_remote, local_ref[0])
    keep_live = jnp.where(forwards, before_live, live_ref[0])

    def arrive(t):
        @pl.when(jnp.logical_or(is_s, t >= split))
        def _():
            direct(t, CHUNK).wait_recv()

        @pl.when(jnp.logical_and(is_r, t < split))
        def _():
            for side in range(2):
                leg2(t, side).wait_recv()

        @pl.when(jnp.logical_and(jnp.logical_and(is_r, t < split), jnp.logical_or(odd == 0, t > 0)))
        def _():
            direct(t, DIRECT).wait_recv()

        @pl.when(jnp.logical_and(r_odd, t == 0))
        def _():
            for k in range(2):
                spec(k).wait_recv()
            direct_rest().wait_recv()
            recv_buf[:SPEC] = jnp.where(remote_ref[0] == 0, spec_buf[0], spec_buf[1])

    def pair(t):
        rows = pl.ds(pl.multiple_of(t * PAIR, PAIR), PAIR)
        gram = lax.dot_general(
            recv_buf[rows],
            xn[keep_index],
            (((1,), (1,)), ((), ())),
            preferred_element_type=jnp.float32,
        )
        pair_acc[...] = jnp.maximum(
            pair_acc[...], jnp.max(gram.reshape(PAIR // 8, 8, BLK), axis=0)
        )
        narrow = gram[:, :128]
        for j in range(1, BLK // 128):
            narrow = jnp.maximum(narrow, gram[:, j * 128 : (j + 1) * 128])
        for j in range(PAIR // 128):
            part = jnp.max(narrow[j * 128 : (j + 1) * 128].T, axis=0, keepdims=True)
            ret_out[pl.ds(t * (PAIR // 128) + j, 1)] = part

    def compare(t, carry):
        for j in range(PAIR // CHUNK):
            arrive(t * (PAIR // CHUNK) + j)
        pair(t)
        return carry

    @pl.when(has_source)
    def _():
        lax.fori_loop(0, BLK // PAIR, compare, 0)

    ret_copy = pltpu.make_async_remote_copy(
        src_ref=ret_out,
        dst_ref=ret_in,
        send_sem=ret_sem.at[0],
        recv_sem=ret_sem.at[1],
        device_id=(source, b),
        device_id_type=MESH,
    )

    @pl.when(has_source)
    def _():
        ret_copy.start()

    @pl.when(has_target)
    def _():
        ret_copy.wait_recv()

    @pl.when(jnp.logical_not(has_target))
    def _():
        ret_in[...] = jnp.full(ret_in.shape, -2.0, jnp.float32)

    kept = jnp.max(pair_acc[...], axis=0, keepdims=True)
    kept = jnp.where(keep_live > 0, kept, -2.0)
    sent = jnp.concatenate([ret_in[t : t + 1] for t in range(ROUNDS)], axis=1)
    sent = jnp.where(send_live > 0, sent, -2.0)
    for k in range(2):
        best = jnp.max(own_acc[k], axis=0, keepdims=True)
        best_ref[k : k + 1] = jnp.maximum(best, jnp.where(keep_index == k, kept, -2.0))
        sent_ref[k : k + 1] = jnp.where(send_index == k, sent, -2.0)

    @pl.when(d < n_dev - 1)
    def _():
        meta_copy.wait_send()

    @pl.when(has_source)
    def _():
        ret_copy.wait_send()

    @pl.when(r_odd)
    def _():
        for side in range(2):
            client(side).wait_send()

    @pl.when(s_odd)
    def _():
        for k in range(2):
            spec(k).wait_send()
        direct_rest().wait_send()

    def drain(t, carry):
        @pl.when(jnp.logical_or(is_r, jnp.logical_and(crosses, t >= split)))
        def _():
            direct(t, CHUNK).wait_send()

        @pl.when(jnp.logical_and(jnp.logical_and(s_cross, odd == 0), t < split))
        def _():
            direct(t, DIRECT).wait_send()

        @pl.when(jnp.logical_and(s_cross, jnp.logical_and(t >= skip, t < split)))
        def _():
            for side in range(2):
                leg1(t, side).wait_send()

        @pl.when(jnp.logical_and(s_odd, t < PRE))
        def _():
            for side in range(2):
                for k in range(2):
                    pre(t, side, k).wait_send()

        @pl.when(jnp.logical_and(s_odd, jnp.logical_and(t > 0, t < split)))
        def _():
            direct(t, DIRECT).wait_send()

        @pl.when(jnp.logical_and(r_cross, t < relayed))
        def _():
            for side in range(2):
                leg2(t, side).wait_send()

        return carry

    lax.fori_loop(0, ROUNDS, drain, 0)


def solution(mesh):
    n_dev, n_band = mesh.shape["dev"], mesh.shape["band"]
    dma = pltpu.SemaphoreType.DMA

    def local(embeddings, pair_local, pair_remote, pair_live):
        blocks = embeddings.reshape(2, BLK, D)
        best, sent = pl.pallas_call(
            functools.partial(kernel, n_dev, n_band),
            out_shape=[jax.ShapeDtypeStruct((2, BLK), jnp.float32)] * 2,
            in_specs=[pl.BlockSpec(memory_space=pltpu.SMEM)] * 3
            + [pl.BlockSpec(memory_space=pl.ANY)],
            out_specs=[pl.BlockSpec(memory_space=pltpu.VMEM)] * 2,
            scratch_shapes=[
                pltpu.VMEM((2, BLK, D), jnp.bfloat16),
                pltpu.VMEM((BLK, D), jnp.bfloat16),
                pltpu.VMEM((BLK, D), jnp.bfloat16),
                pltpu.VMEM((2, ROUNDS * RELAY, D), jnp.bfloat16),
                pltpu.VMEM((2, 2, PRE * RELAY, D), jnp.bfloat16),
                pltpu.VMEM((2, SPEC, D), jnp.bfloat16),
                pltpu.VMEM((2, 8, 128), jnp.int32),
                pltpu.VMEM((8, 128), jnp.int32),
                pltpu.VMEM((8, 128), jnp.int32),
                pltpu.VMEM((ROUNDS, CHUNK), jnp.float32),
                pltpu.VMEM((ROUNDS, CHUNK), jnp.float32),
                pltpu.VMEM((2, 8, BLK), jnp.float32),
                pltpu.VMEM((8, BLK), jnp.float32),
                dma((ROUNDS,)),
                dma((2,)),
                dma((2,)),
                dma((ROUNDS,)),
                dma((ROUNDS,)),
                dma((2, ROUNDS)),
                dma((2, ROUNDS)),
                dma((2, ROUNDS)),
                dma((2, ROUNDS)),
                dma((2, 2, PRE)),
                dma((2, 2, PRE)),
                dma((2,)),
                dma((2,)),
                dma((2,)),
                dma((2,)),
            ],
            compiler_params=pltpu.CompilerParams(
                collective_id=1, has_side_effects=True, vmem_limit_bytes=52 << 20
            ),
            cost_estimate=pl.CostEstimate(
                flops=6 * BLK * BLK * D, bytes_accessed=4 * BLK * D, transcendentals=0
            ),
        )(pair_local, pair_remote, pair_live, blocks)
        return jnp.maximum(best, sent)

    placed = (P(("band", "dev"), None), P(("band", "dev")), P(("band", "dev")), P(("band", "dev")))
    return jax.shard_map(
        local, mesh=mesh, in_specs=placed, out_specs=P(("band", "dev"), None), check_vma=False
    )
```

```python
import functools

import jax
import jax.numpy as jnp
from jax import lax
from jax.experimental import pallas as pl
from jax.experimental.pallas import tpu as pltpu
from jax.sharding import PartitionSpec as P

BLK = 1024
D = 1024
ROUNDS = 8
CHUNK = BLK // ROUNDS
DIRECT = 64
RELAY = 32
SPLIT_EVEN = 6
SPLIT_ODD = 6
SPEC = 48
PRE = 1
OWN = 256
LINE = 8
AHEAD = 6
BEFORE = 4
PAIR = 256
MESH = pl.DeviceIdType.MESH


def kernel(
    n_dev,
    n_band,
    local_ref,
    remote_ref,
    live_ref,
    x_hbm,
    best_ref,
    sent_ref,
    xn,
    send_buf,
    recv_buf,
    relay_buf,
    pre_buf,
    spec_buf,
    client_in,
    meta_out,
    meta_in,
    ret_out,
    ret_in,
    own_acc,
    pair_acc,
    load_sem,
    meta_sem,
    ret_sem,
    direct_send,
    direct_recv,
    leg1_send,
    leg1_recv,
    leg2_send,
    leg2_recv,
    pre_send,
    pre_recv,
    spec_send,
    spec_recv,
    client_send,
    client_recv,
):
    d = lax.axis_index("dev")
    b = lax.axis_index("band")
    c = d % 2
    odd = b % 2
    step = 1 - 2 * odd
    is_s = c == 1 - odd
    is_r = c == odd
    crosses = jnp.where(c == 1, d < n_dev - 1, d > 0)
    s_cross = jnp.logical_and(is_s, crosses)
    r_cross = jnp.logical_and(is_r, crosses)
    s_odd = jnp.logical_and(s_cross, odd == 1)
    r_odd = jnp.logical_and(r_cross, odd == 1)
    r_even = jnp.logical_and(r_cross, odd == 0)
    split = jnp.where(odd == 1, SPLIT_ODD, SPLIT_EVEN)
    skip = jnp.where(odd == 1, PRE, 0)
    relayed = jnp.where(odd == 1, SPLIT_EVEN, SPLIT_ODD)
    other = d + 1 - 2 * c
    across = jnp.where(crosses, d - 1 + 2 * c, other)
    target = jnp.clip(d + step, 0, n_dev - 1)
    source = jnp.clip(d - step, 0, n_dev - 1)
    bands = (lax.rem(b + 1, n_band), lax.rem(b + n_band - 1, n_band))
    has_target = jnp.logical_or(is_r, crosses)
    has_source = jnp.logical_or(is_s, crosses)

    def load(t):
        rows = pl.ds(pl.multiple_of(t * CHUNK, CHUNK), CHUNK)
        return pltpu.make_async_copy(x_hbm.at[:, rows], xn.at[:, rows], load_sem.at[t])

    for t in range(ROUNDS):
        load(t).start()

    barrier = pltpu.get_barrier_semaphore()

    def greet(dev, band):
        pl.semaphore_signal(barrier, inc=1, device_id=(dev, band), device_id_type=MESH)

    greet(other, b)

    @pl.when(crosses)
    def _():
        greet(across, b)

    @pl.when(r_cross)
    def _():
        for band in bands:
            greet(d, band)
            greet(across, band)

    own_acc[...] = jnp.full(own_acc.shape, -2.0, jnp.float32)
    pair_acc[...] = jnp.full(pair_acc.shape, -2.0, jnp.float32)

    def normalize(t, carry):
        rows = pl.ds(pl.multiple_of(t * CHUNK, CHUNK), CHUNK)
        load(t).wait()
        for k in range(2):
            values = xn[k, rows].astype(jnp.float32)
            scale = lax.rsqrt(jnp.sum(values * values, axis=1, keepdims=True) + 1e-06)
            xn[k, rows] = (values * scale).astype(jnp.bfloat16)
        return carry

    first = d // 2 % LINE == 0
    early = jnp.where(first, ROUNDS, 0)
    before = jnp.where(first, BEFORE, 0)
    lax.fori_loop(0, early, normalize, 0)

    row = lax.broadcasted_iota(jnp.int32, (8, 128), 0)
    meta_out[...] = jnp.where(row == 0, remote_ref[0], live_ref[0])

    def own(t, carry):
        k = t % 2
        start = pl.multiple_of(t // 2 * OWN, OWN)
        gram = lax.dot_general(
            xn[k, pl.ds(start, OWN)],
            xn[k],
            (((1,), (1,)), ((), ())),
            preferred_element_type=jnp.float32,
        )
        rows = lax.broadcasted_iota(jnp.int32, gram.shape, 0) + start
        columns = lax.broadcasted_iota(jnp.int32, gram.shape, 1)
        gram = jnp.where(rows == columns, -2.0, gram)
        own_acc[k] = jnp.maximum(own_acc[k], jnp.max(gram.reshape(OWN // 8, 8, BLK), axis=0))
        return carry

    lax.fori_loop(0, before, own, 0)

    waits = 1 + jnp.where(crosses, 3, 0)
    pl.semaphore_wait(barrier, waits)

    meta_copy = pltpu.make_async_remote_copy(
        src_ref=meta_out,
        dst_ref=meta_in,
        send_sem=meta_sem.at[0],
        recv_sem=meta_sem.at[1],
        device_id=(jnp.minimum(d + 1, n_dev - 1), b),
        device_id_type=MESH,
    )

    @pl.when(d < n_dev - 1)
    def _():
        meta_copy.start()

    def client(side):
        return pltpu.make_async_remote_copy(
            src_ref=meta_out,
            dst_ref=client_in.at[side],
            send_sem=client_send.at[side],
            recv_sem=client_recv.at[side],
            device_id=(across, bands[side]),
            device_id_type=MESH,
        )

    @pl.when(r_odd)
    def _():
        for side in range(2):
            client(side).start()

    def piece(t, start, size):
        return pl.ds(pl.multiple_of(t * CHUNK + start, 16), size)

    def direct(t, size):
        rows = piece(t, 0, size)
        return pltpu.make_async_remote_copy(
            src_ref=send_buf.at[rows],
            dst_ref=recv_buf.at[rows],
            send_sem=direct_send.at[t],
            recv_sem=direct_recv.at[t],
            device_id=(target, b),
            device_id_type=MESH,
        )

    def relay_rows(t, side):
        return piece(t, DIRECT + side * RELAY, RELAY)

    def leg1(t, side):
        return pltpu.make_async_remote_copy(
            src_ref=send_buf.at[relay_rows(t, side)],
            dst_ref=relay_buf.at[side, pl.ds(pl.multiple_of(t * RELAY, RELAY), RELAY)],
            send_sem=leg1_send.at[side, t],
            recv_sem=leg1_recv.at[side, t],
            device_id=(d, bands[side]),
            device_id_type=MESH,
        )

    def leg2(t, side):
        return pltpu.make_async_remote_copy(
            src_ref=relay_buf.at[side, pl.ds(pl.multiple_of(t * RELAY, RELAY), RELAY)],
            dst_ref=recv_buf.at[relay_rows(t, side)],
            send_sem=leg2_send.at[side, t],
            recv_sem=leg2_recv.at[side, t],
            device_id=(across, bands[1 - side]),
            device_id_type=MESH,
        )

    def held(t):
        return pl.ds(pl.multiple_of(t * RELAY, RELAY), RELAY)

    def pre(t, side, k):
        return pltpu.make_async_remote_copy(
            src_ref=xn.at[k, relay_rows(t, side)],
            dst_ref=pre_buf.at[side, k, held(t)],
            send_sem=pre_send.at[side, k, t],
            recv_sem=pre_recv.at[side, k, t],
            device_id=(d, bands[side]),
            device_id_type=MESH,
        )

    def spec(k):
        return pltpu.make_async_remote_copy(
            src_ref=xn.at[k, pl.ds(0, SPEC)],
            dst_ref=spec_buf.at[k],
            send_sem=spec_send.at[k],
            recv_sem=spec_recv.at[k],
            device_id=(target, b),
            device_id_type=MESH,
        )

    def direct_rest():
        rows = pl.ds(SPEC, DIRECT - SPEC)
        return pltpu.make_async_remote_copy(
            src_ref=send_buf.at[rows],
            dst_ref=recv_buf.at[rows],
            send_sem=direct_send.at[0],
            recv_sem=direct_recv.at[0],
            device_id=(target, b),
            device_id_type=MESH,
        )

    def forward(t):
        @pl.when(jnp.logical_or(odd == 1, t >= PRE))
        def _():
            for side in range(2):
                leg1(t, side).wait_recv()
                leg2(t, side).start()

        @pl.when(jnp.logical_and(odd == 0, t < PRE))
        def _():
            for side in range(2):
                for k in range(2):
                    pre(t, side, k).wait_recv()
                relay_buf[side, held(t)] = jnp.where(
                    client_in[side, 0, 0] == 0,
                    pre_buf[side, 0, held(t)],
                    pre_buf[side, 1, held(t)],
                )
                leg2(t, side).start()

    def send(t, index):
        rows = piece(t, 0, CHUNK)
        send_buf[rows] = jnp.where(index == 0, xn[0, rows], xn[1, rows])

        @pl.when(is_r)
        def _():
            direct(t, CHUNK).start()

        @pl.when(jnp.logical_and(s_cross, t >= split))
        def _():
            direct(t, CHUNK).start()

        @pl.when(jnp.logical_and(s_cross, jnp.logical_and(t >= skip, t < split)))
        def _():
            for side in range(2):
                leg1(t, side).start()

        @pl.when(jnp.logical_and(jnp.logical_and(s_cross, odd == 0), t < split))
        def _():
            direct(t, DIRECT).start()

        @pl.when(jnp.logical_and(s_odd, t == 0))
        def _():
            direct_rest().start()

        @pl.when(jnp.logical_and(s_odd, jnp.logical_and(t > 0, t < split)))
        def _():
            direct(t, DIRECT).start()

    def send_all(index):
        def body(t, carry):
            @pl.when(jnp.logical_and(jnp.logical_not(s_odd), t >= early))
            def _():
                normalize(t, 0)

            send(t, index)
            return carry

        lax.fori_loop(0, ROUNDS, body, 0)

    def learn():
        @pl.when(d > 0)
        def _():
            meta_copy.wait_recv()

        @pl.when(d == 0)
        def _():
            meta_in[...] = jnp.zeros_like(meta_in)

    def relay(t, carry):
        @pl.when(t >= before)
        def _():
            own(t, 0)

        @pl.when(jnp.logical_and(r_cross, t < relayed))
        def _():
            forward(t)

        return carry

    ahead = jnp.where(jnp.logical_and(is_r, jnp.logical_and(odd == 1, first)), AHEAD, 0)
    lax.fori_loop(0, ahead, relay, 0)

    @pl.when(odd == 0)
    def _():
        send_all(local_ref[0])

    def send_both(t, carry):
        @pl.when(t >= early)
        def _():
            normalize(t, 0)

        @pl.when(t == 0)
        def _():
            for k in range(2):
                spec(k).start()

        @pl.when(t < PRE)
        def _():
            for side in range(2):
                for k in range(2):
                    pre(t, side, k).start()

        return carry

    @pl.when(s_odd)
    def _():
        lax.fori_loop(0, ROUNDS, send_both, 0)

    @pl.when(odd == 1)
    def _():
        learn()
        send_all(meta_in[0, 0])

    @pl.when(r_even)
    def _():
        for side in range(2):
            client(side).wait_recv()

    lax.fori_loop(ahead, ROUNDS, relay, 0)

    @pl.when(odd == 0)
    def _():
        learn()

    before_remote = meta_in[0, 0]
    before_live = meta_in[1, 0]
    forwards = odd == 0
    send_index = jnp.where(forwards, local_ref[0], before_remote)
    send_live = jnp.where(forwards, live_ref[0], before_live)
    keep_index = jnp.where(forwards, before_remote, local_ref[0])
    keep_live = jnp.where(forwards, before_live, live_ref[0])

    def arrive(t):
        @pl.when(jnp.logical_or(is_s, t >= split))
        def _():
            direct(t, CHUNK).wait_recv()

        @pl.when(jnp.logical_and(is_r, t < split))
        def _():
            for side in range(2):
                leg2(t, side).wait_recv()

        @pl.when(jnp.logical_and(jnp.logical_and(is_r, t < split), jnp.logical_or(odd == 0, t > 0)))
        def _():
            direct(t, DIRECT).wait_recv()

        @pl.when(jnp.logical_and(r_odd, t == 0))
        def _():
            for k in range(2):
                spec(k).wait_recv()
            direct_rest().wait_recv()
            recv_buf[:SPEC] = jnp.where(remote_ref[0] == 0, spec_buf[0], spec_buf[1])

    def pair(t):
        rows = pl.ds(pl.multiple_of(t * PAIR, PAIR), PAIR)
        gram = lax.dot_general(
            recv_buf[rows],
            xn[keep_index],
            (((1,), (1,)), ((), ())),
            preferred_element_type=jnp.float32,
        )
        pair_acc[...] = jnp.maximum(
            pair_acc[...], jnp.max(gram.reshape(PAIR // 8, 8, BLK), axis=0)
        )
        narrow = gram[:, :128]
        for j in range(1, BLK // 128):
            narrow = jnp.maximum(narrow, gram[:, j * 128 : (j + 1) * 128])
        for j in range(PAIR // 128):
            part = jnp.max(narrow[j * 128 : (j + 1) * 128].T, axis=0, keepdims=True)
            ret_out[pl.ds(t * (PAIR // 128) + j, 1)] = part

    def compare(t, carry):
        for j in range(PAIR // CHUNK):
            arrive(t * (PAIR // CHUNK) + j)
        pair(t)
        return carry

    @pl.when(has_source)
    def _():
        lax.fori_loop(0, BLK // PAIR, compare, 0)

    ret_copy = pltpu.make_async_remote_copy(
        src_ref=ret_out,
        dst_ref=ret_in,
        send_sem=ret_sem.at[0],
        recv_sem=ret_sem.at[1],
        device_id=(source, b),
        device_id_type=MESH,
    )

    @pl.when(has_source)
    def _():
        ret_copy.start()

    kept = jnp.max(pair_acc[...], axis=0, keepdims=True)
    kept = jnp.where(keep_live > 0, kept, -2.0)
    for k in range(2):
        best = jnp.max(own_acc[k], axis=0, keepdims=True)
        best_ref[k : k + 1] = jnp.maximum(best, jnp.where(keep_index == k, kept, -2.0))

    @pl.when(d < n_dev - 1)
    def _():
        meta_copy.wait_send()

    @pl.when(r_odd)
    def _():
        for side in range(2):
            client(side).wait_send()

    @pl.when(s_odd)
    def _():
        for k in range(2):
            spec(k).wait_send()
        direct_rest().wait_send()

    def drain(t, carry):
        @pl.when(jnp.logical_or(is_r, jnp.logical_and(crosses, t >= split)))
        def _():
            direct(t, CHUNK).wait_send()

        @pl.when(jnp.logical_and(jnp.logical_and(s_cross, odd == 0), t < split))
        def _():
            direct(t, DIRECT).wait_send()

        @pl.when(jnp.logical_and(s_cross, jnp.logical_and(t >= skip, t < split)))
        def _():
            for side in range(2):
                leg1(t, side).wait_send()

        @pl.when(jnp.logical_and(s_odd, t < PRE))
        def _():
            for side in range(2):
                for k in range(2):
                    pre(t, side, k).wait_send()

        @pl.when(jnp.logical_and(s_odd, jnp.logical_and(t > 0, t < split)))
        def _():
            direct(t, DIRECT).wait_send()

        @pl.when(jnp.logical_and(r_cross, t < relayed))
        def _():
            for side in range(2):
                leg2(t, side).wait_send()

        return carry

    lax.fori_loop(0, ROUNDS, drain, 0)

    @pl.when(has_target)
    def _():
        ret_copy.wait_recv()

    @pl.when(jnp.logical_not(has_target))
    def _():
        ret_in[...] = jnp.full(ret_in.shape, -2.0, jnp.float32)

    sent = jnp.concatenate([ret_in[t : t + 1] for t in range(ROUNDS)], axis=1)
    sent = jnp.where(send_live > 0, sent, -2.0)
    for k in range(2):
        sent_ref[k : k + 1] = jnp.where(send_index == k, sent, -2.0)

    @pl.when(has_source)
    def _():
        ret_copy.wait_send()


def solution(mesh):
    n_dev, n_band = mesh.shape["dev"], mesh.shape["band"]
    dma = pltpu.SemaphoreType.DMA

    def local(embeddings, pair_local, pair_remote, pair_live):
        blocks = embeddings.reshape(2, BLK, D)
        best, sent = pl.pallas_call(
            functools.partial(kernel, n_dev, n_band),
            out_shape=[jax.ShapeDtypeStruct((2, BLK), jnp.float32)] * 2,
            in_specs=[pl.BlockSpec(memory_space=pltpu.SMEM)] * 3
            + [pl.BlockSpec(memory_space=pl.ANY)],
            out_specs=[pl.BlockSpec(memory_space=pltpu.VMEM)] * 2,
            scratch_shapes=[
                pltpu.VMEM((2, BLK, D), jnp.bfloat16),
                pltpu.VMEM((BLK, D), jnp.bfloat16),
                pltpu.VMEM((BLK, D), jnp.bfloat16),
                pltpu.VMEM((2, ROUNDS * RELAY, D), jnp.bfloat16),
                pltpu.VMEM((2, 2, PRE * RELAY, D), jnp.bfloat16),
                pltpu.VMEM((2, SPEC, D), jnp.bfloat16),
                pltpu.VMEM((2, 8, 128), jnp.int32),
                pltpu.VMEM((8, 128), jnp.int32),
                pltpu.VMEM((8, 128), jnp.int32),
                pltpu.VMEM((ROUNDS, CHUNK), jnp.float32),
                pltpu.VMEM((ROUNDS, CHUNK), jnp.float32),
                pltpu.VMEM((2, 8, BLK), jnp.float32),
                pltpu.VMEM((8, BLK), jnp.float32),
                dma((ROUNDS,)),
                dma((2,)),
                dma((2,)),
                dma((ROUNDS,)),
                dma((ROUNDS,)),
                dma((2, ROUNDS)),
                dma((2, ROUNDS)),
                dma((2, ROUNDS)),
                dma((2, ROUNDS)),
                dma((2, 2, PRE)),
                dma((2, 2, PRE)),
                dma((2,)),
                dma((2,)),
                dma((2,)),
                dma((2,)),
            ],
            compiler_params=pltpu.CompilerParams(
                collective_id=1, has_side_effects=True, vmem_limit_bytes=52 << 20
            ),
            cost_estimate=pl.CostEstimate(
                flops=6 * BLK * BLK * D, bytes_accessed=4 * BLK * D, transcendentals=0
            ),
        )(pair_local, pair_remote, pair_live, blocks)
        return jnp.maximum(best, sent)

    placed = (P(("band", "dev"), None), P(("band", "dev")), P(("band", "dev")), P(("band", "dev")))
    return jax.shard_map(
        local, mesh=mesh, in_specs=placed, out_specs=P(("band", "dev"), None), check_vma=False
    )
```
